32 devices in a mesh: parts: 2 (over y), seg: 4 (over z), grp: 4 (over x, core).
Axes of the slice: x: 2, y: 2, z: 4, core: 2. Of those that a mesh axis runs over, the one named last changes fastest.
Arguments:
- env_left: bfloat16 [8, 4, 30, 192, 192], P(('parts', 'seg'), 'grp'), parts along dimension 0, may hold values from -1 to 2
- env_right: bfloat16 [8, 4, 30, 192, 192], P(('parts', 'seg'), 'grp'), parts along dimension 0, may hold values from -1 to 2
- site_left: bfloat16 [8, 4, 192, 192], P(('parts', 'seg'), 'grp'), parts along dimension 0, may hold values from -6 to 6
- site_right: bfloat16 [8, 4, 192, 192], P(('parts', 'seg'), 'grp'), parts along dimension 0, may hold values from -2 to 2
- bond_weights: float32 [8, 4, 192], P(('parts', 'seg'), 'grp'), parts along dimension 0, may hold values from 0.5 to 2
- mpo_charge: int32 [8, 30], P(('parts', 'seg')), parts along dimension 0, may hold values from -1 to 1, as said below
- sector_rows: int32 [8, 4], P(('parts', 'seg'), 'grp'), parts along dimension 0, may hold values from 1 to 192, 576 in all within a row
Outputs:
- theta_new: float32 [8, 4, 192, 192], P(('parts', 'seg'), 'grp'), parts along dimension 0
- energy: float32 [8], P(('parts', 'seg')), parts along dimension 0
The draws below stay inside these ranges and needn't reach their ends.
There are 2 independent parts, one for each index of `parts`. The reference program is written for one: setup_inputs(seed, part) draws one part's arguments, and reference() takes and returns one part's arrays. A program takes and returns all parts, laid end to end along the dimension named above; each array names one. Nothing has to cross between parts.
Inputs may be any that keep to these rules, and one draw needn't show every extreme that they name: `sector_rows`: for each segment the 4 values sum to 576 and the largest is 192. `mpo_charge`: for each segment exactly 10 of the 30 values are -1, exactly 10 are +1, the rest 0.
All inputs are finite; a program needn't handle non-finite values. No bound on the sum of `sector_rows` on one device may be relied on, other than what follows from the above.
Results may differ from the reference program's by a relative error of at most 0.0054.
Values may be sent and summed in bfloat16 or wider, within the bound.
A program may use at most 64 MiB of HBM per device.

```python
import math
import jax
import jax.numpy as jnp
import numpy as np
from jax import lax

BLK = 192
W = 30
CHG = 10
NSEG = 4
NSEC = 4


def draw_mpo_charge(key, part):
    seg_keys = jax.random.split(jax.random.fold_in(key, 17), NSEG)
    orders = jax.vmap(lambda one_key: jax.random.permutation(one_key, W))(seg_keys)
    charges = jnp.where(orders < CHG, -1, jnp.where(orders < 2 * CHG, 1, 0))
    return charges.astype(jnp.int32)


def blend_parts(common, own, share):
    return math.sqrt(share) * common + math.sqrt(1.0 - share) * own


def shifted_block(noise, diag_value):
    eye_block = jnp.eye(BLK, dtype=jnp.float32)
    return diag_value * eye_block + 0.5 * noise / math.sqrt(BLK)


def draw_env_left(key, part):
    key = jax.random.fold_in(key, 31)
    shape = (NSEG, NSEC, W, BLK, BLK)
    noise = jnp.clip(jax.random.normal(key, shape, jnp.float32), -4.0, 4.0)
    diag_value = 0.5
    return shifted_block(noise, diag_value).astype(jnp.bfloat16)


def draw_env_right(key, part):
    key = jax.random.fold_in(key, 37)
    shape = (NSEG, NSEC, W, BLK, BLK)
    noise = jnp.clip(jax.random.normal(key, shape, jnp.float32), -4.0, 4.0)
    diag_value = 0.5
    return shifted_block(noise, diag_value).astype(jnp.bfloat16)


def draw_site_left(key, part):
    key = jax.random.fold_in(key, 23)
    common_key, own_key = jax.random.split(key)
    common = jnp.clip(jax.random.normal(common_key, (NSEG, 1, BLK, BLK), jnp.float32), -4.0, 4.0)
    own = jnp.clip(jax.random.normal(own_key, (NSEG, NSEC, BLK, BLK), jnp.float32), -4.0, 4.0)
    share = 0.65
    return blend_parts(common, own, share).astype(jnp.bfloat16)


def draw_site_right(key, part):
    key = jax.random.fold_in(key, 29)
    common_key, own_key = jax.random.split(key)
    common = jnp.clip(jax.random.normal(common_key, (NSEG, 1, BLK, BLK), jnp.float32), -4.0, 4.0)
    own = jnp.clip(jax.random.normal(own_key, (NSEG, NSEC, BLK, BLK), jnp.float32), -4.0, 4.0)
    share = 0.65
    return (blend_parts(common, own, share) / math.sqrt(BLK)).astype(jnp.bfloat16)


def shard_levels(key, shape, pieces, smallest, high):
    factor_of = 1.0
    for axis_at, shards_of in pieces:
        steps = jax.random.uniform(jax.random.fold_in(jax.random.fold_in(key, 6), axis_at), (shards_of,), jnp.float32, smallest / len(pieces), high / len(pieces))
        factor_of = factor_of * jnp.repeat(jnp.exp(steps), shape[axis_at] // shards_of).reshape((-1,) + (1,) * (len(shape) - 1 - axis_at))
    return factor_of


def profile(count, total, most, slope):
    loads = [(1 << 20) // math.isqrt(grade ** slope) + 1 for grade in range(2, count + 1)]
    surplus, given = total - most - (count - 1), [1] * (count - 1)
    while surplus > 0:
        movable = [i for i in range(count - 1) if given[i] < most]
        whole, remaining = sum([loads[i] for i in movable]), surplus
        for i in movable:
            extra = min(most - given[i], max(1, remaining * loads[i] // whole), surplus)
            given[i] = given[i] + extra
            surplus = surplus - extra
    return np.array([most] + given)


def uneven(key, amount, total, limit, slope):
    if amount == 2:
        one = jax.random.randint(key, (), max(1, total - limit), min(limit, total - 1) + 1)
        return jnp.stack([one, total - one])
    lengths = jnp.asarray(profile(amount, total, limit, slope), jnp.int32)
    pairs = (amount - 1) // 2
    source_of, receiver = lengths[1:1 + 2 * pairs:2], lengths[2:2 + 2 * pairs:2]
    room = jnp.minimum(source_of - 1, limit - receiver)
    moved = jax.random.randint(jax.random.fold_in(key, 1), (pairs,), 0, 1 << 20) % (room + 1)
    lengths = lengths.at[1:1 + 2 * pairs:2].set(source_of - moved).at[2:2 + 2 * pairs:2].set(receiver + moved)
    return lengths[jax.random.permutation(jax.random.fold_in(key, 2), amount)]


def setup_inputs(seed: int = 0, part: int = 0) -> dict:
    arg_keys = jax.random.split(jax.random.key(seed), 8)
    part_splits = jax.random.split(jax.random.fold_in(arg_keys[7], part), 8)
    env_left = draw_env_left(jax.random.fold_in(jax.random.fold_in(arg_keys[7], part), 71), part)
    env_right = draw_env_right(jax.random.fold_in(jax.random.fold_in(arg_keys[7], part), 71), part)
    site_left = draw_site_left(jax.random.fold_in(jax.random.fold_in(arg_keys[7], part), 71), part)
    site_right = draw_site_right(jax.random.fold_in(jax.random.fold_in(arg_keys[7], part), 71), part)
    bond_weights = jnp.clip(jnp.exp(math.log(2.0) - 1.3862944 * jax.random.uniform(part_splits[4], (NSEG, NSEC, BLK), jnp.float32) ** shard_levels(part_splits[4], (NSEG, NSEC, BLK), ((0, 4), (1, 4)), -0.2, 0.2)), 0.5, 2.0)
    mpo_charge = draw_mpo_charge(jax.random.fold_in(jax.random.fold_in(arg_keys[7], part), 71), part)
    sector_rows = jax.vmap(lambda own: uneven(own, NSEC, 3 * NSEC * BLK // 4, BLK, 2))(jax.random.split(part_splits[6], NSEG)).reshape((NSEG, NSEC)).astype(jnp.int32)
    return {"env_left": env_left, "env_right": env_right, "site_left": site_left, "site_right": site_right, "bond_weights": bond_weights, "mpo_charge": mpo_charge, "sector_rows": sector_rows}


eps_value = 1e-06
highest = lax.Precision.HIGHEST

def one_segment(left_env, edge_tensor, right_env, site_right, charges, rows):
    live_rows = (jnp.arange(BLK, dtype=jnp.int32)[None, :, None] < rows[:, None, None]).astype(jnp.float32)
    theta_vec = jnp.einsum('qab,qbc->qac', edge_tensor.astype(jnp.float32), site_right.astype(jnp.float32), precision=highest) * live_rows
    entry_count = jnp.float32(NSEC * BLK * BLK)
    sector_ids = jnp.arange(NSEC, dtype=jnp.int32)
    chosen = (sector_ids[:, None, None] + charges[None, :, None] == sector_ids[None, None, :]).astype(jnp.float32)
    left_wide = left_env.astype(jnp.float32)
    right_wide = right_env.astype(jnp.float32)

    def matvec(vector):
        rounded = lax.optimization_barrier(vector.astype(jnp.bfloat16)).astype(jnp.float32)
        inner_prod = jnp.einsum('qwab,qbc->qwac', left_wide, rounded, precision=highest)
        inner_prod = lax.optimization_barrier(inner_prod.astype(jnp.bfloat16)).astype(jnp.float32)
        outer_prod = jnp.einsum('qwac,qwcd->qwad', inner_prod, right_wide, precision=highest)
        partial_value = jnp.einsum('qwp,qwad->qpad', chosen, outer_prod, precision=highest)
        partial_value = lax.optimization_barrier(partial_value.astype(jnp.bfloat16)).astype(jnp.float32)
        return lax.optimization_barrier(jnp.sum(partial_value, axis=0)) * live_rows

    def product(first_vec, second_vec):
        return jnp.sum(first_vec * second_vec) / entry_count
    basis_one = theta_vec / jnp.sqrt(product(theta_vec, theta_vec) + eps_value)
    image_one = matvec(basis_one)
    diag_one = product(basis_one, image_one)
    residual = image_one - diag_one * basis_one
    res_norm = product(residual, residual)
    basis_two = residual / jnp.sqrt(res_norm + eps_value)
    image_two = matvec(basis_two)
    coupling = product(basis_two, image_one)
    diag_two = product(basis_two, image_two)
    half_gap = 0.5 * (diag_one - diag_two)
    energy = 0.5 * (diag_one + diag_two) - jnp.sqrt(half_gap * half_gap + coupling * coupling)
    lead_coef = diag_two - energy
    norm_scale = jnp.sqrt(lead_coef * lead_coef + coupling * coupling)
    theta_new = (lead_coef * basis_one - coupling * basis_two) / norm_scale
    return (theta_new, energy)

def reference(env_left, env_right, site_left, site_right, bond_weights, mpo_charge, sector_rows):
    scaled = (site_left.astype(jnp.float32) / bond_weights[:, :, None, :]).astype(jnp.bfloat16)
    eye_block = jnp.eye(BLK, dtype=jnp.bfloat16)
    vacuum_one = jnp.where(jnp.arange(W, dtype=jnp.int32)[:, None, None] == 0, eye_block[None], jnp.zeros((1, BLK, BLK), jnp.bfloat16))
    vacuum = jnp.broadcast_to(vacuum_one[None], (NSEC, W, BLK, BLK))
    edge_eye = jnp.broadcast_to(eye_block[None], (NSEC, BLK, BLK))
    thetas = []
    energies = []
    for segment in range(NSEG):
        if segment == 0:
            left_env, edge_tensor = (vacuum, edge_eye)
        else:
            left_env, edge_tensor = (env_left[segment - 1], scaled[segment - 1])
        theta_new, energy = one_segment(left_env, edge_tensor, env_right[segment], site_right[segment], mpo_charge[segment], sector_rows[segment])
        thetas.append(theta_new)
        energies.append(energy)
    return (jnp.stack(thetas), jnp.stack(energies))
```

```python
import functools

import jax
import jax.numpy as jnp
from jax import lax
from jax.experimental import pallas as pl
from jax.experimental.pallas import tpu as pltpu
from jax.sharding import PartitionSpec as P

eps_value = 1e-06
lanes = 128
f32 = jnp.float32
bf16 = jnp.bfloat16


def pack(dst, x):
    size = x.shape[0]
    half, rest = size // 2, size - lanes
    dst[0:size, :] = x[:, :lanes]
    dst[size : size + half, :] = jnp.concatenate([x[:half, lanes:], x[half:, lanes:]], axis=1)


def unpack(src, size):
    half, rest = size // 2, size - lanes
    tail = src[size : size + half, :]
    tall = jnp.concatenate([tail[:, :rest], tail[:, rest:]], axis=0)
    return jnp.concatenate([src[0:size, :], tall], axis=1)


def kernel(
    segs, grps, chunk,
    el, er, sl, sr, bw, chg, rows,
    theta_out, energy_out,
    elv, erv, send_a, send_b, recv_a, recv_b, full_a, full_b,
    site_send, site_recv, ch_loc, ch_rem,
    theta, v16, image, acc,
    slab_send, slab_recv, z_send, z_recv, res_send, res_recv,
    stat_send, stat_recv, low_send, low_recv,
    loc_sem, env_s, env_r, site_s, site_r, slab_s, slab_r,
    z_s, z_r, res_s, res_r, stat_s, stat_r, low_s, low_r,
):
    width, size, _ = el.shape
    half = width // 2
    chunks = half // chunk
    entry_count = float(grps * size * size)
    s = lax.axis_index("seg")
    q = lax.axis_index("grp")
    has_up = s < segs - 1
    has_dn = s > 0
    has_hi = q < grps - 1
    has_lo = q > 0
    up, dn = jnp.minimum(s + 1, segs - 1), jnp.maximum(s - 1, 0)
    hi, lo = jnp.minimum(q + 1, grps - 1), jnp.maximum(q - 1, 0)
    upper, lower = 0, 1

    def remote(src, dst, ssem, rsem, **where):
        return pltpu.make_async_remote_copy(
            src_ref=src, dst_ref=dst, send_sem=ssem, recv_sem=rsem,
            device_id=where, device_id_type=pl.DeviceIdType.MESH,
        )

    def load_a(k):
        at = pl.ds(k * chunk, chunk)
        return pltpu.make_async_copy(el.at[at], elv.at[at], loc_sem.at[k])

    def load_b(k):
        at = pl.ds(half + k * chunk, chunk)
        return pltpu.make_async_copy(er.at[at], erv.at[at], loc_sem.at[chunks + k])

    def load_rest_a():
        at = pl.ds(half, half)
        return pltpu.make_async_copy(el.at[at], elv.at[at], loc_sem.at[2 * chunks])

    def load_rest_b():
        at = pl.ds(0, half)
        return pltpu.make_async_copy(er.at[at], erv.at[at], loc_sem.at[2 * chunks + 1])

    for k in range(chunks):
        load_a(k).start()
        load_b(k).start()
    load_rest_a().start()
    load_rest_b().start()

    barrier = pltpu.get_barrier_semaphore()
    for d in range(1, grps):
        pl.semaphore_signal(
            barrier, inc=1, device_id={"grp": lax.rem(q + d, grps)},
            device_id_type=pl.DeviceIdType.MESH)

    @pl.when(has_up)
    def _():
        for j in range(grps):
            pl.semaphore_signal(
                barrier, inc=1, device_id={"seg": up, "grp": j},
                device_id_type=pl.DeviceIdType.MESH)

    @pl.when(has_dn)
    def _():
        for j in range(grps):
            pl.semaphore_signal(
                barrier, inc=1, device_id={"seg": dn, "grp": j},
                device_id_type=pl.DeviceIdType.MESH)

    scaled = (sl[...].astype(f32) / bw[...]).astype(bf16)
    site_right = sr[...]
    pack(site_send.at[0], scaled)
    pack(site_send.at[1], site_right)
    for w in range(width):
        ch_loc[w : w + 1, :] = jnp.full((1, size), chg[0, w], jnp.int32).astype(f32)
    pad = ch_loc.shape[0] - width
    ch_loc[width:, :] = jnp.full((pad, size), rows[0, 0], jnp.int32).astype(f32)

    pl.semaphore_wait(
        barrier, grps - 1 + grps * (has_up.astype(jnp.int32) + has_dn.astype(jnp.int32)))

    def site_up():
        return remote(site_send.at[0], site_recv.at[0], site_s.at[0], site_r.at[0], seg=up)

    def site_dn():
        return remote(site_send.at[1], site_recv.at[1], site_s.at[1], site_r.at[1], seg=dn)

    def ch_dn():
        return remote(ch_loc, ch_rem, site_s.at[2], site_r.at[2], seg=dn)

    def env_up(k):
        return remote(send_a.at[k], recv_a.at[k], env_s.at[0, k], env_r.at[0, k], seg=up)

    def env_dn(k):
        return remote(send_b.at[k], recv_b.at[k], env_s.at[1, k], env_r.at[1, k], seg=dn)

    @pl.when(has_up)
    def _():
        site_up().start()

    @pl.when(has_dn)
    def _():
        site_dn().start()
        ch_dn().start()

    def send_chunk(k, carry):
        load_a(k).wait()
        load_b(k).wait()

        @pl.when(has_up)
        def _():
            for j in range(chunk):
                pack(send_a.at[k, j], elv[k * chunk + j])
            env_up(k).start()

        @pl.when(has_dn)
        def _():
            for j in range(chunk):
                pack(send_b.at[k, j], erv[half + k * chunk + j])
            env_dn(k).start()

        return carry

    lax.fori_loop(0, chunks, send_chunk, 0)
    load_rest_a().wait()
    load_rest_b().wait()

    row_at = lax.broadcasted_iota(jnp.int32, (size, size), 0)
    col_at = lax.broadcasted_iota(jnp.int32, (size, size), 1)
    eye_block = jnp.where(row_at == col_at, 1.0, 0.0)

    @pl.when(jnp.logical_not(has_dn))
    def _():
        for w in range(half):
            full_a[w] = (eye_block if w == 0 else jnp.zeros_like(eye_block)).astype(bf16)

    row_f = row_at.astype(f32)

    def live(ch):
        return jnp.where(row_f < ch[width : width + 1, :], 1.0, 0.0)

    @pl.when(has_dn)
    def _():
        site_up().wait_recv()
        edge = unpack(site_recv.at[0], size)
        theta[upper] = jnp.dot(edge, site_right, preferred_element_type=f32) * live(ch_loc)

    @pl.when(jnp.logical_not(has_dn))
    def _():
        theta[upper] = site_right.astype(f32) * live(ch_loc)

    @pl.when(has_up)
    def _():
        site_dn().wait_recv()
        ch_dn().wait_recv()
        above = unpack(site_recv.at[1], size)
        theta[lower] = jnp.dot(scaled, above, preferred_element_type=f32) * live(ch_rem)

    @pl.when(jnp.logical_not(has_up))
    def _():
        theta[lower] = jnp.zeros((size, size), f32)

    def column_sums(x):
        return jnp.sum(x, axis=0, keepdims=True)

    def stat_copy(slot, d):
        return remote(
            stat_send.at[slot], stat_recv.at[slot, q], stat_s.at[slot, d], stat_r.at[slot, d],
            grp=lax.rem(q + d, grps))

    def stat_tile(values):
        at = lax.broadcasted_iota(jnp.int32, (8, size), 0)
        tile = jnp.zeros((8, size), f32)
        for i, value in enumerate(values):
            tile = jnp.where(at == i, value, tile)
        return tile

    def stat_start(slot, values):
        tile = stat_tile(values)
        stat_send[slot] = tile
        stat_recv[slot, q] = tile
        for d in range(1, grps):
            stat_copy(slot, d).start()

    def total(tiles, extra=None):
        tile = tiles[0]
        for j in range(1, grps):
            tile = tile + tiles[j]
        if extra is not None:
            for j in range(grps):
                tile = tile + extra[j]
        return jnp.sum(tile, axis=1, keepdims=True) / entry_count

    def stat_finish(slot):
        for d in range(1, grps):
            stat_copy(slot, d).wait_recv()
        return stat_recv.at[slot]

    stat_start(0, [column_sums(theta[i] * theta[i]) for i in (upper, lower)])
    norms = total(stat_finish(0))
    for i in (upper, lower):
        basis = theta[i] / jnp.sqrt(norms[i : i + 1, :] + eps_value)
        theta[i] = basis
        v16[i] = basis.astype(bf16)
        acc[i] = jnp.zeros(acc.shape[1:], f32)

    def one_term(a, v, ch_row, b):
        inner = jnp.dot(a, v, preferred_element_type=f32).astype(bf16)
        parts = [inner * jnp.where(ch_row == c, 1.0, 0.0).astype(bf16) for c in (-1.0, 0.0, 1.0)]
        return jnp.dot(jnp.concatenate(parts, axis=0), b, preferred_element_type=f32)

    def upper_chunk(k):
        value = None
        for j in range(chunk):
            w = k * chunk + j
            term = one_term(full_a[w], v16[upper], ch_loc[pl.ds(w, 1), :], erv[w])
            value = term if value is None else value + term
        acc[upper] = acc[upper] + value

    def lower_chunk(k):
        value = None
        for j in range(chunk):
            w = k * chunk + j
            term = one_term(elv[half + w], v16[lower], ch_rem[pl.ds(half + w, 1), :], full_b[w])
            value = term if value is None else value + term
        acc[lower] = acc[lower] + value

    def first_chunk(k, carry):
        @pl.when(has_dn)
        def _():
            env_up(k).wait_recv()
            for j in range(chunk):
                full_a[k * chunk + j] = unpack(recv_a.at[k, j], size)

        upper_chunk(k)

        @pl.when(has_up)
        def _():
            env_dn(k).wait_recv()
            for j in range(chunk):
                full_b[k * chunk + j] = unpack(recv_b.at[k, j], size)
            lower_chunk(k)

        return carry

    lax.fori_loop(0, chunks, first_chunk, 0)

    def slab_copy(role, way):
        return remote(
            slab_send.at[role, way], slab_recv.at[role, way], slab_s.at[role, way],
            slab_r.at[role, way], grp=(lo, hi)[way])

    def res_copy(role, way):
        return remote(
            res_send.at[role], res_recv.at[role, way], res_s.at[role, way],
            res_r.at[role, way], grp=(lo, hi)[way])

    def z_copy(role):
        return remote(
            z_send.at[role], z_recv.at[1 - role], z_s.at[role], z_r.at[1 - role],
            seg=(dn, up)[role])

    def z_incoming(role):
        return remote(
            z_send.at[role], z_recv.at[role], z_s.at[role], z_r.at[role],
            seg=(dn, up)[role])

    def slab(role, c):
        return acc[role, c * size : (c + 1) * size, :]

    def send_slabs(role):
        @pl.when(has_lo)
        def _():
            pack(slab_send.at[role, 0], slab(role, 0).astype(bf16))
            slab_copy(role, 0).start()

        @pl.when(has_hi)
        def _():
            pack(slab_send.at[role, 1], slab(role, 2).astype(bf16))
            slab_copy(role, 1).start()

    def join_slabs(role, ch):
        image[role] = slab(role, 1).astype(bf16).astype(f32)

        @pl.when(has_hi)
        def _():
            slab_copy(role, 0).wait_recv()
            image[role] = image[role] + unpack(slab_recv.at[role, 0], size).astype(f32)

        @pl.when(has_lo)
        def _():
            slab_copy(role, 1).wait_recv()
            image[role] = image[role] + unpack(slab_recv.at[role, 1], size).astype(f32)

        half_image = (image[role] * live(ch)).astype(bf16)
        pack(z_send.at[role], half_image)
        z_copy(role).start()
        image[role] = half_image.astype(f32)

    send_slabs(upper)

    @pl.when(has_up)
    def _():
        send_slabs(lower)

    @pl.when(has_dn)
    def _():
        join_slabs(upper, ch_loc)

    @pl.when(jnp.logical_not(has_dn))
    def _():
        image[upper] = slab(upper, 1).astype(bf16).astype(f32)

        @pl.when(has_hi)
        def _():
            slab_copy(upper, 0).wait_recv()
            image[upper] = image[upper] + unpack(slab_recv.at[upper, 0], size).astype(f32)

        @pl.when(has_lo)
        def _():
            slab_copy(upper, 1).wait_recv()
            image[upper] = image[upper] + unpack(slab_recv.at[upper, 1], size).astype(f32)

        image[upper] = image[upper] * live(ch_loc)

    @pl.when(has_up)
    def _():
        join_slabs(lower, ch_rem)

    @pl.when(jnp.logical_not(has_up))
    def _():
        image[lower] = jnp.zeros((size, size), f32)

    @pl.when(has_dn)
    def _():
        z_incoming(upper).wait_recv()
        image[upper] = image[upper] + unpack(z_recv.at[upper], size).astype(f32)

    @pl.when(has_up)
    def _():
        z_incoming(lower).wait_recv()
        image[lower] = image[lower] + unpack(z_recv.at[lower], size).astype(f32)

    stat_start(1, [column_sums(theta[i] * image[i]) for i in (upper, lower)])
    diags = total(stat_finish(1))
    diag_one = diags[0:1, :]

    def send_res(role):
        residual = image[role] - diags[role : role + 1, :] * theta[role]
        rounded = residual.astype(bf16)
        v16[role] = rounded
        pack(res_send.at[role], rounded)

        @pl.when(has_lo)
        def _():
            res_copy(role, 0).start()

        @pl.when(has_hi)
        def _():
            res_copy(role, 1).start()

        return residual

    residual = send_res(upper)

    @pl.when(has_up)
    def _():
        send_res(lower)

    for i in (upper, lower):
        acc[i] = jnp.zeros(acc.shape[1:], f32)

    def second_chunk(k, carry):
        upper_chunk(k)

        @pl.when(has_up)
        def _():
            lower_chunk(k)

        return carry

    lax.fori_loop(0, chunks, second_chunk, 0)

    def overlap(role, own):
        theta_out[...] = own * slab(role, 1)

        @pl.when(has_hi)
        def _():
            res_copy(role, 0).wait_recv()
            above = unpack(res_recv.at[role, 0], size).astype(f32)
            theta_out[...] = theta_out[...] + above * slab(role, 2)

        @pl.when(has_lo)
        def _():
            res_copy(role, 1).wait_recv()
            below = unpack(res_recv.at[role, 1], size).astype(f32)
            theta_out[...] = theta_out[...] + below * slab(role, 0)

        return column_sums(theta_out[...])

    def low_copy(j):
        return remote(
            low_send, low_recv.at[q], low_s.at[j], low_r.at[q], seg=up, grp=j)

    def low_incoming(j):
        return remote(low_send, low_recv.at[j], low_s.at[j], low_r.at[j], seg=dn, grp=j)

    @pl.when(has_up)
    def _():
        zero = jnp.zeros((1, size), f32)
        low_send[...] = stat_tile([zero, zero, overlap(lower, v16[lower].astype(f32))])
        for j in range(grps):
            low_copy(j).start()

    stat_start(
        2,
        [
            column_sums(residual * residual),
            column_sums(residual * image[upper]),
            overlap(upper, residual),
        ],
    )

    @pl.when(has_dn)
    def _():
        for j in range(grps):
            low_incoming(j).wait_recv()

    @pl.when(jnp.logical_not(has_dn))
    def _():
        low_recv[...] = jnp.zeros(low_recv.shape, f32)

    sums = total(stat_finish(2), low_recv)
    scale = 1.0 / jnp.sqrt(sums[0:1, :] + eps_value)
    coupling = sums[1:2, :] * scale
    diag_two = sums[2:3, :] * scale * scale
    half_gap = 0.5 * (diag_one - diag_two)
    energy = 0.5 * (diag_one + diag_two) - jnp.sqrt(half_gap * half_gap + coupling * coupling)
    lead_coef = diag_two - energy
    norm_scale = jnp.sqrt(lead_coef * lead_coef + coupling * coupling)
    energy_out[...] = energy
    theta_out[...] = (lead_coef * theta[upper] - coupling * (residual * scale)) / norm_scale

    @pl.when(has_up)
    def _():
        site_up().wait_send()
        z_copy(lower).wait_send()
        for k in range(chunks):
            env_up(k).wait_send()
        for j in range(grps):
            low_copy(j).wait_send()

    @pl.when(has_dn)
    def _():
        site_dn().wait_send()
        ch_dn().wait_send()
        z_copy(upper).wait_send()
        for k in range(chunks):
            env_dn(k).wait_send()

    for slot in range(3):
        for d in range(1, grps):
            stat_copy(slot, d).wait_send()

    def drain(role):
        @pl.when(has_lo)
        def _():
            slab_copy(role, 0).wait_send()
            res_copy(role, 0).wait_send()

        @pl.when(has_hi)
        def _():
            slab_copy(role, 1).wait_send()
            res_copy(role, 1).wait_send()

    drain(upper)

    @pl.when(has_up)
    def _():
        drain(lower)


def body(env_left, env_right, site_left, site_right, bond_weights, mpo_charge, sector_rows):
    width, size = env_left.shape[2:4]
    segs, grps = lax.axis_size("seg"), lax.axis_size("grp")
    half = width // 2
    chunk = 3 if half % 3 == 0 else 1
    chunks = half // chunk
    tall = size + size // 2
    charge_rows = (width // 8 + 1) * 8
    vmem = pl.BlockSpec(memory_space=pltpu.VMEM)
    smem = pl.BlockSpec(memory_space=pltpu.SMEM)
    hbm = pl.BlockSpec(memory_space=pl.ANY)
    dma = pltpu.SemaphoreType.DMA
    theta_new, energy = pl.pallas_call(
        functools.partial(kernel, segs, grps, chunk),
        out_shape=(
            jax.ShapeDtypeStruct((size, size), f32),
            jax.ShapeDtypeStruct((1, 1), f32),
        ),
        in_specs=[hbm, hbm, vmem, vmem, vmem, smem, smem],
        out_specs=(vmem, vmem),
        scratch_shapes=[
            pltpu.VMEM((width, size, size), bf16),
            pltpu.VMEM((width, size, size), bf16),
            pltpu.VMEM((chunks, chunk, tall, lanes), bf16),
            pltpu.VMEM((chunks, chunk, tall, lanes), bf16),
            pltpu.VMEM((chunks, chunk, tall, lanes), bf16),
            pltpu.VMEM((chunks, chunk, tall, lanes), bf16),
            pltpu.VMEM((half, size, size), bf16),
            pltpu.VMEM((half, size, size), bf16),
            pltpu.VMEM((2, tall, lanes), bf16),
            pltpu.VMEM((2, tall, lanes), bf16),
            pltpu.VMEM((charge_rows, size), f32),
            pltpu.VMEM((charge_rows, size), f32),
            pltpu.VMEM((2, size, size), f32),
            pltpu.VMEM((2, size, size), bf16),
            pltpu.VMEM((2, size, size), f32),
            pltpu.VMEM((2, 3 * size, size), f32),
            pltpu.VMEM((2, 2, tall, lanes), bf16),
            pltpu.VMEM((2, 2, tall, lanes), bf16),
            pltpu.VMEM((2, tall, lanes), bf16),
            pltpu.VMEM((2, tall, lanes), bf16),
            pltpu.VMEM((2, tall, lanes), bf16),
            pltpu.VMEM((2, 2, tall, lanes), bf16),
            pltpu.VMEM((3, 8, size), f32),
            pltpu.VMEM((3, grps, 8, size), f32),
            pltpu.VMEM((8, size), f32),
            pltpu.VMEM((grps, 8, size), f32),
            dma((2 * chunks + 2,)),
            dma((2, chunks)),
            dma((2, chunks)),
            dma((3,)),
            dma((3,)),
            dma((2, 2)),
            dma((2, 2)),
            dma((2,)),
            dma((2,)),
            dma((2, 2)),
            dma((2, 2)),
            dma((3, grps)),
            dma((3, grps)),
            dma((grps,)),
            dma((grps,)),
        ],
        compiler_params=pltpu.CompilerParams(
            collective_id=0, has_side_effects=True, vmem_limit_bytes=40 * 1024 * 1024
        ),
        cost_estimate=pl.CostEstimate(
            flops=16 * width * size**3, bytes_accessed=4 * width * size * size, transcendentals=0
        ),
    )(
        env_left[0, 0],
        env_right[0, 0],
        site_left[0, 0],
        site_right[0, 0],
        bond_weights[0],
        mpo_charge,
        sector_rows,
    )
    return (theta_new[None, None], energy[0])


def solution(mesh):
    return jax.shard_map(
        body,
        mesh=mesh,
        in_specs=(
            P(("parts", "seg"), "grp", None, None, None),
            P(("parts", "seg"), "grp", None, None, None),
            P(("parts", "seg"), "grp", None, None),
            P(("parts", "seg"), "grp", None, None),
            P(("parts", "seg"), "grp", None),
            P(("parts", "seg"), None),
            P(("parts", "seg"), "grp"),
        ),
        out_specs=(P(("parts", "seg"), "grp", None, None), P(("parts", "seg"))),
        check_vma=False,
    )
```

```python
import functools

import jax
import jax.numpy as jnp
from jax import lax
from jax.experimental import pallas as pl
from jax.experimental.pallas import tpu as pltpu
from jax.sharding import PartitionSpec as P

eps_value = 1e-06
lanes = 128
f32 = jnp.float32
bf16 = jnp.bfloat16


def pack(dst, x):
    size = x.shape[0]
    half, rest = size // 2, size - lanes
    dst[0:size, :] = x[:, :lanes]
    dst[size : size + half, :] = jnp.concatenate([x[:half, lanes:], x[half:, lanes:]], axis=1)


def unpack(src, size):
    half, rest = size // 2, size - lanes
    tail = src[size : size + half, :]
    tall = jnp.concatenate([tail[:, :rest], tail[:, rest:]], axis=0)
    return jnp.concatenate([src[0:size, :], tall], axis=1)


def kernel(
    segs, grps, chunk,
    el, er, sl_in, sr_in, bw_in, chg_in, rows_in,
    theta_out, energy_out,
    sl, sr, bw, chg, rows, elv, erv, send_a, send_b, recv_a, recv_b, full_a, full_b,
    site_send, site_recv, ch_loc, ch_rem,
    theta, v16, image, acc,
    slab_send, slab_recv, z_send, z_recv, res_send, res_recv,
    stat_send, stat_recv, low_send, low_recv,
    loc_sem, env_s, env_r, site_s, site_r, slab_s, slab_r,
    z_s, z_r, res_s, res_r, stat_s, stat_r, low_s, low_r,
):
    width, size, _ = el.shape
    half = width // 2
    chunks = half // chunk
    entry_count = float(grps * size * size)
    s = lax.axis_index("seg")
    q = lax.axis_index("grp")
    has_up = s < segs - 1
    has_dn = s > 0
    has_hi = q < grps - 1
    has_lo = q > 0
    up, dn = jnp.minimum(s + 1, segs - 1), jnp.maximum(s - 1, 0)
    hi, lo = jnp.minimum(q + 1, grps - 1), jnp.maximum(q - 1, 0)
    upper, lower = 0, 1

    def remote(src, dst, ssem, rsem, **where):
        return pltpu.make_async_remote_copy(
            src_ref=src, dst_ref=dst, send_sem=ssem, recv_sem=rsem,
            device_id=where, device_id_type=pl.DeviceIdType.MESH,
        )

    def load_a(k):
        at = pl.ds(k * chunk, chunk)
        return pltpu.make_async_copy(el.at[at], elv.at[at], loc_sem.at[k])

    def load_b(k):
        at = pl.ds(half + k * chunk, chunk)
        return pltpu.make_async_copy(er.at[at], erv.at[at], loc_sem.at[chunks + k])

    def load_rest_a():
        at = pl.ds(half, half)
        return pltpu.make_async_copy(el.at[at], elv.at[at], loc_sem.at[2 * chunks])

    def load_rest_b():
        at = pl.ds(0, half)
        return pltpu.make_async_copy(er.at[at], erv.at[at], loc_sem.at[2 * chunks + 1])

    small = [
        pltpu.make_async_copy(src, dst, loc_sem.at[2 * chunks + 2 + i])
        for i, (src, dst) in enumerate(
            ((sl_in, sl), (bw_in, bw), (sr_in, sr), (chg_in, chg), (rows_in, rows)))
    ]
    for copy in small:
        copy.start()
    for k in range(chunks):
        load_a(k).start()
        load_b(k).start()
    load_rest_a().start()
    load_rest_b().start()

    barrier = pltpu.get_barrier_semaphore()
    for d in range(1, grps):
        pl.semaphore_signal(
            barrier, inc=1, device_id={"grp": lax.rem(q + d, grps)},
            device_id_type=pl.DeviceIdType.MESH)

    @pl.when(has_up)
    def _():
        for j in range(grps):
            pl.semaphore_signal(
                barrier, inc=1, device_id={"seg": up, "grp": j},
                device_id_type=pl.DeviceIdType.MESH)

    @pl.when(has_dn)
    def _():
        for j in range(grps):
            pl.semaphore_signal(
                barrier, inc=1, device_id={"seg": dn, "grp": j},
                device_id_type=pl.DeviceIdType.MESH)

    for copy in small:
        copy.wait()
    scaled = (sl[...].astype(f32) / bw[...]).astype(bf16)
    site_right = sr[...]
    pack(site_send.at[0], scaled)
    pack(site_send.at[1], site_right)
    for w in range(width):
        ch_loc[w : w + 1, :] = jnp.full((1, size), chg[0, w], jnp.int32).astype(f32)
    pad = ch_loc.shape[0] - width
    ch_loc[width:, :] = jnp.full((pad, size), rows[0, 0], jnp.int32).astype(f32)

    pl.semaphore_wait(
        barrier, grps - 1 + grps * (has_up.astype(jnp.int32) + has_dn.astype(jnp.int32)))

    def site_up():
        return remote(site_send.at[0], site_recv.at[0], site_s.at[0], site_r.at[0], seg=up)

    def site_dn():
        return remote(site_send.at[1], site_recv.at[1], site_s.at[1], site_r.at[1], seg=dn)

    def ch_dn():
        return remote(ch_loc, ch_rem, site_s.at[2], site_r.at[2], seg=dn)

    def env_up(k):
        return remote(send_a.at[k], recv_a.at[k], env_s.at[0, k], env_r.at[0, k], seg=up)

    def env_dn(k):
        return remote(send_b.at[k], recv_b.at[k], env_s.at[1, k], env_r.at[1, k], seg=dn)

    @pl.when(has_up)
    def _():
        site_up().start()

    @pl.when(has_dn)
    def _():
        site_dn().start()
        ch_dn().start()

    def send_chunk(k, carry):
        load_a(k).wait()
        load_b(k).wait()

        @pl.when(has_up)
        def _():
            for j in range(chunk):
                pack(send_a.at[k, j], elv[k * chunk + j])
            env_up(k).start()

        @pl.when(has_dn)
        def _():
            for j in range(chunk):
                pack(send_b.at[k, j], erv[half + k * chunk + j])
            env_dn(k).start()

        return carry

    lax.fori_loop(0, chunks, send_chunk, 0)
    load_rest_a().wait()
    load_rest_b().wait()

    row_at = lax.broadcasted_iota(jnp.int32, (size, size), 0)
    col_at = lax.broadcasted_iota(jnp.int32, (size, size), 1)
    eye_block = jnp.where(row_at == col_at, 1.0, 0.0)

    @pl.when(jnp.logical_not(has_dn))
    def _():
        for w in range(half):
            full_a[w] = (eye_block if w == 0 else jnp.zeros_like(eye_block)).astype(bf16)

    row_f = row_at.astype(f32)

    def live(ch):
        return jnp.where(row_f < ch[width : width + 1, :], 1.0, 0.0)

    @pl.when(has_dn)
    def _():
        site_up().wait_recv()
        edge = unpack(site_recv.at[0], size)
        theta[upper] = jnp.dot(edge, site_right, preferred_element_type=f32) * live(ch_loc)

    @pl.when(jnp.logical_not(has_dn))
    def _():
        theta[upper] = site_right.astype(f32) * live(ch_loc)

    @pl.when(has_up)
    def _():
        site_dn().wait_recv()
        ch_dn().wait_recv()
        above = unpack(site_recv.at[1], size)
        theta[lower] = jnp.dot(scaled, above, preferred_element_type=f32) * live(ch_rem)

    @pl.when(jnp.logical_not(has_up))
    def _():
        theta[lower] = jnp.zeros((size, size), f32)

    def column_sums(x):
        return jnp.sum(x, axis=0, keepdims=True)

    def stat_copy(slot, d):
        return remote(
            stat_send.at[slot], stat_recv.at[slot, q], stat_s.at[slot, d], stat_r.at[slot, d],
            grp=lax.rem(q + d, grps))

    def stat_tile(values):
        at = lax.broadcasted_iota(jnp.int32, (8, size), 0)
        tile = jnp.zeros((8, size), f32)
        for i, value in enumerate(values):
            tile = jnp.where(at == i, value, tile)
        return tile

    def stat_start(slot, values):
        tile = stat_tile(values)
        stat_send[slot] = tile
        stat_recv[slot, q] = tile
        for d in range(1, grps):
            stat_copy(slot, d).start()

    def total(tiles, extra=None):
        tile = tiles[0]
        for j in range(1, grps):
            tile = tile + tiles[j]
        if extra is not None:
            for j in range(grps):
                tile = tile + extra[j]
        return jnp.sum(tile, axis=1, keepdims=True) / entry_count

    def stat_finish(slot):
        for d in range(1, grps):
            stat_copy(slot, d).wait_recv()
        return stat_recv.at[slot]

    stat_start(0, [column_sums(theta[i] * theta[i]) for i in (upper, lower)])
    norms = total(stat_finish(0))
    for i in (upper, lower):
        basis = theta[i] / jnp.sqrt(norms[i : i + 1, :] + eps_value)
        theta[i] = basis
        v16[i] = basis.astype(bf16)
        acc[i] = jnp.zeros(acc.shape[1:], f32)

    def one_term(a, v, ch_row, b):
        inner = jnp.dot(a, v, preferred_element_type=f32).astype(bf16)
        parts = [inner * jnp.where(ch_row == c, 1.0, 0.0).astype(bf16) for c in (-1.0, 0.0, 1.0)]
        return jnp.dot(jnp.concatenate(parts, axis=0), b, preferred_element_type=f32)

    def upper_chunk(k):
        value = None
        for j in range(chunk):
            w = k * chunk + j
            term = one_term(full_a[w], v16[upper], ch_loc[pl.ds(w, 1), :], erv[w])
            value = term if value is None else value + term
        acc[upper] = acc[upper] + value

    def lower_chunk(k):
        value = None
        for j in range(chunk):
            w = k * chunk + j
            term = one_term(elv[half + w], v16[lower], ch_rem[pl.ds(half + w, 1), :], full_b[w])
            value = term if value is None else value + term
        acc[lower] = acc[lower] + value

    def first_chunk(k, carry):
        @pl.when(has_dn)
        def _():
            env_up(k).wait_recv()
            for j in range(chunk):
                full_a[k * chunk + j] = unpack(recv_a.at[k, j], size)

        upper_chunk(k)

        @pl.when(has_up)
        def _():
            env_dn(k).wait_recv()
            for j in range(chunk):
                full_b[k * chunk + j] = unpack(recv_b.at[k, j], size)
            lower_chunk(k)

        return carry

    lax.fori_loop(0, chunks, first_chunk, 0)

    def slab_copy(role, way):
        return remote(
            slab_send.at[role, way], slab_recv.at[role, way], slab_s.at[role, way],
            slab_r.at[role, way], grp=(lo, hi)[way])

    def res_copy(role, way):
        return remote(
            res_send.at[role], res_recv.at[role, way], res_s.at[role, way],
            res_r.at[role, way], grp=(lo, hi)[way])

    def z_copy(role):
        return remote(
            z_send.at[role], z_recv.at[1 - role], z_s.at[role], z_r.at[1 - role],
            seg=(dn, up)[role])

    def z_incoming(role):
        return remote(
            z_send.at[role], z_recv.at[role], z_s.at[role], z_r.at[role],
            seg=(dn, up)[role])

    def slab(role, c):
        return acc[role, c * size : (c + 1) * size, :]

    def send_slabs(role):
        @pl.when(has_lo)
        def _():
            pack(slab_send.at[role, 0], slab(role, 0).astype(bf16))
            slab_copy(role, 0).start()

        @pl.when(has_hi)
        def _():
            pack(slab_send.at[role, 1], slab(role, 2).astype(bf16))
            slab_copy(role, 1).start()

    def join_slabs(role, ch):
        image[role] = slab(role, 1).astype(bf16).astype(f32)

        @pl.when(has_hi)
        def _():
            slab_copy(role, 0).wait_recv()
            image[role] = image[role] + unpack(slab_recv.at[role, 0], size).astype(f32)

        @pl.when(has_lo)
        def _():
            slab_copy(role, 1).wait_recv()
            image[role] = image[role] + unpack(slab_recv.at[role, 1], size).astype(f32)

        half_image = (image[role] * live(ch)).astype(bf16)
        pack(z_send.at[role], half_image)
        z_copy(role).start()
        image[role] = half_image.astype(f32)

    send_slabs(upper)

    @pl.when(has_up)
    def _():
        send_slabs(lower)

    @pl.when(has_dn)
    def _():
        join_slabs(upper, ch_loc)

    @pl.when(jnp.logical_not(has_dn))
    def _():
        image[upper] = slab(upper, 1).astype(bf16).astype(f32)

        @pl.when(has_hi)
        def _():
            slab_copy(upper, 0).wait_recv()
            image[upper] = image[upper] + unpack(slab_recv.at[upper, 0], size).astype(f32)

        @pl.when(has_lo)
        def _():
            slab_copy(upper, 1).wait_recv()
            image[upper] = image[upper] + unpack(slab_recv.at[upper, 1], size).astype(f32)

        image[upper] = image[upper] * live(ch_loc)

    @pl.when(has_up)
    def _():
        join_slabs(lower, ch_rem)

    @pl.when(jnp.logical_not(has_up))
    def _():
        image[lower] = jnp.zeros((size, size), f32)

    @pl.when(has_dn)
    def _():
        z_incoming(upper).wait_recv()
        image[upper] = image[upper] + unpack(z_recv.at[upper], size).astype(f32)

    @pl.when(has_up)
    def _():
        z_incoming(lower).wait_recv()
        image[lower] = image[lower] + unpack(z_recv.at[lower], size).astype(f32)

    stat_start(1, [column_sums(theta[i] * image[i]) for i in (upper, lower)])
    diags = total(stat_finish(1))
    diag_one = diags[0:1, :]

    def send_res(role):
        residual = image[role] - diags[role : role + 1, :] * theta[role]
        rounded = residual.astype(bf16)
        v16[role] = rounded
        pack(res_send.at[role], rounded)

        @pl.when(has_lo)
        def _():
            res_copy(role, 0).start()

        @pl.when(has_hi)
        def _():
            res_copy(role, 1).start()

        return residual

    residual = send_res(upper)

    @pl.when(has_up)
    def _():
        send_res(lower)

    for i in (upper, lower):
        acc[i] = jnp.zeros(acc.shape[1:], f32)

    def second_chunk(k, carry):
        upper_chunk(k)

        @pl.when(has_up)
        def _():
            lower_chunk(k)

        return carry

    lax.fori_loop(0, chunks, second_chunk, 0)

    def overlap(role, own):
        theta_out[...] = own * slab(role, 1)

        @pl.when(has_hi)
        def _():
            res_copy(role, 0).wait_recv()
            above = unpack(res_recv.at[role, 0], size).astype(f32)
            theta_out[...] = theta_out[...] + above * slab(role, 2)

        @pl.when(has_lo)
        def _():
            res_copy(role, 1).wait_recv()
            below = unpack(res_recv.at[role, 1], size).astype(f32)
            theta_out[...] = theta_out[...] + below * slab(role, 0)

        return column_sums(theta_out[...])

    def low_copy(j):
        return remote(
            low_send, low_recv.at[q], low_s.at[j], low_r.at[q], seg=up, grp=j)

    def low_incoming(j):
        return remote(low_send, low_recv.at[j], low_s.at[j], low_r.at[j], seg=dn, grp=j)

    @pl.when(has_up)
    def _():
        zero = jnp.zeros((1, size), f32)
        low_send[...] = stat_tile([zero, zero, overlap(lower, v16[lower].astype(f32))])
        for j in range(grps):
            low_copy(j).start()

    stat_start(
        2,
        [
            column_sums(residual * residual),
            column_sums(residual * image[upper]),
            overlap(upper, residual),
        ],
    )

    @pl.when(has_dn)
    def _():
        for j in range(grps):
            low_incoming(j).wait_recv()

    @pl.when(jnp.logical_not(has_dn))
    def _():
        low_recv[...] = jnp.zeros(low_recv.shape, f32)

    sums = total(stat_finish(2), low_recv)
    scale = 1.0 / jnp.sqrt(sums[0:1, :] + eps_value)
    coupling = sums[1:2, :] * scale
    diag_two = sums[2:3, :] * scale * scale
    half_gap = 0.5 * (diag_one - diag_two)
    energy = 0.5 * (diag_one + diag_two) - jnp.sqrt(half_gap * half_gap + coupling * coupling)
    lead_coef = diag_two - energy
    norm_scale = jnp.sqrt(lead_coef * lead_coef + coupling * coupling)
    energy_out[...] = energy
    theta_out[...] = (lead_coef * theta[upper] - coupling * (residual * scale)) / norm_scale

    @pl.when(has_up)
    def _():
        site_up().wait_send()
        z_copy(lower).wait_send()
        for k in range(chunks):
            env_up(k).wait_send()
        for j in range(grps):
            low_copy(j).wait_send()

    @pl.when(has_dn)
    def _():
        site_dn().wait_send()
        ch_dn().wait_send()
        z_copy(upper).wait_send()
        for k in range(chunks):
            env_dn(k).wait_send()

    for slot in range(3):
        for d in range(1, grps):
            stat_copy(slot, d).wait_send()

    def drain(role):
        @pl.when(has_lo)
        def _():
            slab_copy(role, 0).wait_send()
            res_copy(role, 0).wait_send()

        @pl.when(has_hi)
        def _():
            slab_copy(role, 1).wait_send()
            res_copy(role, 1).wait_send()

    drain(upper)

    @pl.when(has_up)
    def _():
        drain(lower)


def body(env_left, env_right, site_left, site_right, bond_weights, mpo_charge, sector_rows):
    width, size = env_left.shape[2:4]
    segs, grps = lax.axis_size("seg"), lax.axis_size("grp")
    half = width // 2
    chunk = 3 if half % 3 == 0 else 1
    chunks = half // chunk
    tall = size + size // 2
    charge_rows = (width // 8 + 1) * 8
    vmem = pl.BlockSpec(memory_space=pltpu.VMEM)
    hbm = pl.BlockSpec(memory_space=pltpu.HBM)
    dma = pltpu.SemaphoreType.DMA
    theta_new, energy = pl.pallas_call(
        functools.partial(kernel, segs, grps, chunk),
        out_shape=(
            jax.ShapeDtypeStruct((size, size), f32),
            jax.ShapeDtypeStruct((1, 1), f32),
        ),
        in_specs=[hbm] * 7,
        out_specs=(vmem, vmem),
        scratch_shapes=[
            pltpu.VMEM((size, size), bf16),
            pltpu.VMEM((size, size), bf16),
            pltpu.VMEM((1, size), f32),
            pltpu.SMEM(mpo_charge.shape, jnp.int32),
            pltpu.SMEM(sector_rows.shape, jnp.int32),
            pltpu.VMEM((width, size, size), bf16),
            pltpu.VMEM((width, size, size), bf16),
            pltpu.VMEM((chunks, chunk, tall, lanes), bf16),
            pltpu.VMEM((chunks, chunk, tall, lanes), bf16),
            pltpu.VMEM((chunks, chunk, tall, lanes), bf16),
            pltpu.VMEM((chunks, chunk, tall, lanes), bf16),
            pltpu.VMEM((half, size, size), bf16),
            pltpu.VMEM((half, size, size), bf16),
            pltpu.VMEM((2, tall, lanes), bf16),
            pltpu.VMEM((2, tall, lanes), bf16),
            pltpu.VMEM((charge_rows, size), f32),
            pltpu.VMEM((charge_rows, size), f32),
            pltpu.VMEM((2, size, size), f32),
            pltpu.VMEM((2, size, size), bf16),
            pltpu.VMEM((2, size, size), f32),
            pltpu.VMEM((2, 3 * size, size), f32),
            pltpu.VMEM((2, 2, tall, lanes), bf16),
            pltpu.VMEM((2, 2, tall, lanes), bf16),
            pltpu.VMEM((2, tall, lanes), bf16),
            pltpu.VMEM((2, tall, lanes), bf16),
            pltpu.VMEM((2, tall, lanes), bf16),
            pltpu.VMEM((2, 2, tall, lanes), bf16),
            pltpu.VMEM((3, 8, size), f32),
            pltpu.VMEM((3, grps, 8, size), f32),
            pltpu.VMEM((8, size), f32),
            pltpu.VMEM((grps, 8, size), f32),
            dma((2 * chunks + 7,)),
            dma((2, chunks)),
            dma((2, chunks)),
            dma((3,)),
            dma((3,)),
            dma((2, 2)),
            dma((2, 2)),
            dma((2,)),
            dma((2,)),
            dma((2, 2)),
            dma((2, 2)),
            dma((3, grps)),
            dma((3, grps)),
            dma((grps,)),
            dma((grps,)),
        ],
        compiler_params=pltpu.CompilerParams(
            collective_id=0, has_side_effects=True, vmem_limit_bytes=62 * 1024 * 1024
        ),
        cost_estimate=pl.CostEstimate(
            flops=16 * width * size**3, bytes_accessed=4 * width * size * size, transcendentals=0
        ),
    )(
        env_left[0, 0],
        env_right[0, 0],
        site_left[0, 0],
        site_right[0, 0],
        bond_weights[0],
        mpo_charge,
        sector_rows,
    )
    return (theta_new[None, None], energy[0])


def solution(mesh):
    return jax.shard_map(
        body,
        mesh=mesh,
        in_specs=(
            P(("parts", "seg"), "grp", None, None, None),
            P(("parts", "seg"), "grp", None, None, None),
            P(("parts", "seg"), "grp", None, None),
            P(("parts", "seg"), "grp", None, None),
            P(("parts", "seg"), "grp", None),
            P(("parts", "seg"), None),
            P(("parts", "seg"), "grp"),
        ),
        out_specs=(P(("parts", "seg"), "grp", None, None), P(("parts", "seg"))),
        check_vma=False,
    )
```

```python
import functools

import jax
import jax.numpy as jnp
from jax import lax
from jax.experimental import pallas as pl
from jax.experimental.pallas import tpu as pltpu
from jax.sharding import PartitionSpec as P

eps_value = 1e-06
lanes = 128
f32 = jnp.float32
bf16 = jnp.bfloat16


def pack(dst, x):
    size = x.shape[0]
    half, rest = size // 2, size - lanes
    dst[0:size, :] = x[:, :lanes]
    dst[size : size + half, :] = jnp.concatenate([x[:half, lanes:], x[half:, lanes:]], axis=1)


def unpack(src, size):
    half, rest = size // 2, size - lanes
    tail = src[size : size + half, :]
    tall = jnp.concatenate([tail[:, :rest], tail[:, rest:]], axis=0)
    return jnp.concatenate([src[0:size, :], tall], axis=1)


def kernel(
    segs, grps, chunk,
    el, er, sl_in, sr_in, bw_in, chg_in, rows_in,
    theta_out, energy_out,
    sl, sr, bw, chg, rows, elv, erv, send_a, send_b, recv_a, recv_b, full_a, full_b,
    site_send, site_recv, ch_loc, ch_rem,
    theta, v16, image, acc,
    slab_send, slab_recv, z_send, z_recv, res_send, res_recv,
    stat_send, stat_recv, low_send, low_recv,
    loc_sem, env_s, env_r, site_s, site_r, slab_s, slab_r,
    z_s, z_r, res_s, res_r, stat_s, stat_r, low_s, low_r,
):
    width, size, _ = el.shape
    half = width // 2
    chunks = half // chunk
    entry_count = float(grps * size * size)
    s = lax.axis_index("seg")
    q = lax.axis_index("grp")
    has_up = s < segs - 1
    has_dn = s > 0
    has_hi = q < grps - 1
    has_lo = q > 0
    up, dn = jnp.minimum(s + 1, segs - 1), jnp.maximum(s - 1, 0)
    hi, lo = jnp.minimum(q + 1, grps - 1), jnp.maximum(q - 1, 0)
    upper, lower = 0, 1

    def remote(src, dst, ssem, rsem, **where):
        return pltpu.make_async_remote_copy(
            src_ref=src, dst_ref=dst, send_sem=ssem, recv_sem=rsem,
            device_id=where, device_id_type=pl.DeviceIdType.MESH,
        )

    def load_a(k):
        at = pl.ds(k * chunk, chunk)
        return pltpu.make_async_copy(el.at[at], elv.at[at], loc_sem.at[k])

    def load_b(k):
        at = pl.ds(half + k * chunk, chunk)
        return pltpu.make_async_copy(er.at[at], erv.at[at], loc_sem.at[chunks + k])

    def load_rest_a():
        at = pl.ds(half, half)
        return pltpu.make_async_copy(el.at[at], elv.at[at], loc_sem.at[2 * chunks])

    def load_rest_b():
        at = pl.ds(0, half)
        return pltpu.make_async_copy(er.at[at], erv.at[at], loc_sem.at[2 * chunks + 1])

    small = [
        pltpu.make_async_copy(src, dst, loc_sem.at[2 * chunks + 2 + i])
        for i, (src, dst) in enumerate(
            ((sl_in, sl), (bw_in, bw), (sr_in, sr), (chg_in, chg), (rows_in, rows)))
    ]
    for copy in small:
        copy.start()
    for k in range(chunks):
        load_a(k).start()
        load_b(k).start()
    load_rest_a().start()
    load_rest_b().start()

    barrier = pltpu.get_barrier_semaphore()
    for d in range(1, grps):
        pl.semaphore_signal(
            barrier, inc=1, device_id={"grp": lax.rem(q + d, grps)},
            device_id_type=pl.DeviceIdType.MESH)

    @pl.when(has_up)
    def _():
        for j in range(grps):
            pl.semaphore_signal(
                barrier, inc=1, device_id={"seg": up, "grp": j},
                device_id_type=pl.DeviceIdType.MESH)

    @pl.when(has_dn)
    def _():
        for j in range(grps):
            pl.semaphore_signal(
                barrier, inc=1, device_id={"seg": dn, "grp": j},
                device_id_type=pl.DeviceIdType.MESH)

    for copy in small:
        copy.wait()
    scaled = (sl[...].astype(f32) / bw[...]).astype(bf16)
    site_right = sr[...]
    pack(site_send.at[0], scaled)
    pack(site_send.at[1], site_right)
    for w in range(width):
        ch_loc[w : w + 1, :] = jnp.full((1, size), chg[0, w], jnp.int32).astype(f32)
    pad = ch_loc.shape[0] - width
    ch_loc[width:, :] = jnp.full((pad, size), rows[0, 0], jnp.int32).astype(f32)

    def pack_chunk(k, carry):
        load_a(k).wait()
        load_b(k).wait()
        for j in range(chunk):
            pack(send_a.at[k, j], elv[k * chunk + j])
            pack(send_b.at[k, j], erv[half + k * chunk + j])
        return carry

    lax.fori_loop(0, chunks, pack_chunk, 0)
    load_rest_a().wait()
    load_rest_b().wait()

    row_at = lax.broadcasted_iota(jnp.int32, (size, size), 0)
    col_at = lax.broadcasted_iota(jnp.int32, (size, size), 1)
    eye_block = jnp.where(row_at == col_at, 1.0, 0.0)

    @pl.when(jnp.logical_not(has_dn))
    def _():
        for w in range(half):
            full_a[w] = (eye_block if w == 0 else jnp.zeros_like(eye_block)).astype(bf16)

    for i in (upper, lower):
        acc[i] = jnp.zeros(acc.shape[1:], f32)

    pl.semaphore_wait(
        barrier, grps - 1 + grps * (has_up.astype(jnp.int32) + has_dn.astype(jnp.int32)))

    def site_up():
        return remote(site_send.at[0], site_recv.at[0], site_s.at[0], site_r.at[0], seg=up)

    def site_dn():
        return remote(site_send.at[1], site_recv.at[1], site_s.at[1], site_r.at[1], seg=dn)

    def ch_dn():
        return remote(ch_loc, ch_rem, site_s.at[2], site_r.at[2], seg=dn)

    def env_up(k):
        return remote(send_a.at[k], recv_a.at[k], env_s.at[0, k], env_r.at[0, k], seg=up)

    def env_dn(k):
        return remote(send_b.at[k], recv_b.at[k], env_s.at[1, k], env_r.at[1, k], seg=dn)

    @pl.when(has_up)
    def _():
        site_up().start()

    @pl.when(has_dn)
    def _():
        site_dn().start()
        ch_dn().start()

    def send_chunk(k, carry):
        @pl.when(has_up)
        def _():
            env_up(k).start()

        @pl.when(has_dn)
        def _():
            env_dn(k).start()

        return carry

    lax.fori_loop(0, chunks, send_chunk, 0)

    row_f = row_at.astype(f32)

    def live(ch):
        return jnp.where(row_f < ch[width : width + 1, :], 1.0, 0.0)

    @pl.when(has_dn)
    def _():
        site_up().wait_recv()
        edge = unpack(site_recv.at[0], size)
        theta[upper] = jnp.dot(edge, site_right, preferred_element_type=f32) * live(ch_loc)

    @pl.when(jnp.logical_not(has_dn))
    def _():
        theta[upper] = site_right.astype(f32) * live(ch_loc)

    @pl.when(has_up)
    def _():
        site_dn().wait_recv()
        ch_dn().wait_recv()
        above = unpack(site_recv.at[1], size)
        theta[lower] = jnp.dot(scaled, above, preferred_element_type=f32) * live(ch_rem)

    @pl.when(jnp.logical_not(has_up))
    def _():
        theta[lower] = jnp.zeros((size, size), f32)

    def column_sums(x):
        return jnp.sum(x, axis=0, keepdims=True)

    def stat_copy(slot, d):
        return remote(
            stat_send.at[slot], stat_recv.at[slot, q], stat_s.at[slot, d], stat_r.at[slot, d],
            grp=lax.rem(q + d, grps))

    def stat_tile(values):
        at = lax.broadcasted_iota(jnp.int32, (8, size), 0)
        tile = jnp.zeros((8, size), f32)
        for i, value in enumerate(values):
            tile = jnp.where(at == i, value, tile)
        return tile

    def stat_start(slot, values):
        tile = stat_tile(values)
        stat_send[slot] = tile
        stat_recv[slot, q] = tile
        for d in range(1, grps):
            stat_copy(slot, d).start()

    def total(tiles, extra=None):
        tile = tiles[0]
        for j in range(1, grps):
            tile = tile + tiles[j]
        if extra is not None:
            for j in range(grps):
                tile = tile + extra[j]
        return jnp.sum(tile, axis=1, keepdims=True) / entry_count

    def stat_finish(slot):
        for d in range(1, grps):
            stat_copy(slot, d).wait_recv()
        return stat_recv.at[slot]

    stat_start(0, [column_sums(theta[i] * theta[i]) for i in (upper, lower)])
    norms = total(stat_finish(0))
    for i in (upper, lower):
        basis = theta[i] / jnp.sqrt(norms[i : i + 1, :] + eps_value)
        theta[i] = basis
        v16[i] = basis.astype(bf16)

    def one_term(a, v, ch_row, b):
        inner = jnp.dot(a, v, preferred_element_type=f32).astype(bf16)
        parts = [inner * jnp.where(ch_row == c, 1.0, 0.0).astype(bf16) for c in (-1.0, 0.0, 1.0)]
        return jnp.dot(jnp.concatenate(parts, axis=0), b, preferred_element_type=f32)

    def upper_chunk(k):
        value = None
        for j in range(chunk):
            w = k * chunk + j
            term = one_term(full_a[w], v16[upper], ch_loc[pl.ds(w, 1), :], erv[w])
            value = term if value is None else value + term
        acc[upper] = acc[upper] + value

    def lower_chunk(k):
        value = None
        for j in range(chunk):
            w = k * chunk + j
            term = one_term(elv[half + w], v16[lower], ch_rem[pl.ds(half + w, 1), :], full_b[w])
            value = term if value is None else value + term
        acc[lower] = acc[lower] + value

    def first_chunk(k, carry):
        @pl.when(has_dn)
        def _():
            env_up(k).wait_recv()
            for j in range(chunk):
                full_a[k * chunk + j] = unpack(recv_a.at[k, j], size)

        upper_chunk(k)

        @pl.when(has_up)
        def _():
            env_dn(k).wait_recv()
            for j in range(chunk):
                full_b[k * chunk + j] = unpack(recv_b.at[k, j], size)
            lower_chunk(k)

        return carry

    lax.fori_loop(0, chunks, first_chunk, 0)

    def slab_copy(role, way):
        return remote(
            slab_send.at[role, way], slab_recv.at[role, way], slab_s.at[role, way],
            slab_r.at[role, way], grp=(lo, hi)[way])

    def res_copy(role, way):
        return remote(
            res_send.at[role], res_recv.at[role, way], res_s.at[role, way],
            res_r.at[role, way], grp=(lo, hi)[way])

    def z_copy(role):
        return remote(
            z_send.at[role], z_recv.at[1 - role], z_s.at[role], z_r.at[1 - role],
            seg=(dn, up)[role])

    def z_incoming(role):
        return remote(
            z_send.at[role], z_recv.at[role], z_s.at[role], z_r.at[role],
            seg=(dn, up)[role])

    def slab(role, c):
        return acc[role, c * size : (c + 1) * size, :]

    def send_slabs(role):
        @pl.when(has_lo)
        def _():
            pack(slab_send.at[role, 0], slab(role, 0).astype(bf16))
            slab_copy(role, 0).start()

        @pl.when(has_hi)
        def _():
            pack(slab_send.at[role, 1], slab(role, 2).astype(bf16))
            slab_copy(role, 1).start()

    def join_slabs(role, ch):
        image[role] = slab(role, 1).astype(bf16).astype(f32)

        @pl.when(has_hi)
        def _():
            slab_copy(role, 0).wait_recv()
            image[role] = image[role] + unpack(slab_recv.at[role, 0], size).astype(f32)

        @pl.when(has_lo)
        def _():
            slab_copy(role, 1).wait_recv()
            image[role] = image[role] + unpack(slab_recv.at[role, 1], size).astype(f32)

        half_image = (image[role] * live(ch)).astype(bf16)
        pack(z_send.at[role], half_image)
        z_copy(role).start()
        image[role] = half_image.astype(f32)

    send_slabs(upper)

    @pl.when(has_up)
    def _():
        send_slabs(lower)

    @pl.when(has_dn)
    def _():
        join_slabs(upper, ch_loc)

    @pl.when(jnp.logical_not(has_dn))
    def _():
        image[upper] = slab(upper, 1).astype(bf16).astype(f32)

        @pl.when(has_hi)
        def _():
            slab_copy(upper, 0).wait_recv()
            image[upper] = image[upper] + unpack(slab_recv.at[upper, 0], size).astype(f32)

        @pl.when(has_lo)
        def _():
            slab_copy(upper, 1).wait_recv()
            image[upper] = image[upper] + unpack(slab_recv.at[upper, 1], size).astype(f32)

        image[upper] = image[upper] * live(ch_loc)

    @pl.when(has_up)
    def _():
        join_slabs(lower, ch_rem)

    @pl.when(jnp.logical_not(has_up))
    def _():
        image[lower] = jnp.zeros((size, size), f32)

    @pl.when(has_dn)
    def _():
        z_incoming(upper).wait_recv()
        image[upper] = image[upper] + unpack(z_recv.at[upper], size).astype(f32)

    @pl.when(has_up)
    def _():
        z_incoming(lower).wait_recv()
        image[lower] = image[lower] + unpack(z_recv.at[lower], size).astype(f32)

    stat_start(1, [column_sums(theta[i] * image[i]) for i in (upper, lower)])
    for i in (upper, lower):
        v16[i] = image[i].astype(bf16)
        acc[i] = jnp.zeros(acc.shape[1:], f32)

    def upper_step(k, carry):
        upper_chunk(k)
        return carry

    def lower_step(k, carry):
        lower_chunk(k)
        return carry

    lax.fori_loop(0, chunks, upper_step, 0)

    diags = total(stat_finish(1))
    diag_one = diags[0:1, :]

    def send_res(role):
        residual = image[role] - diags[role : role + 1, :] * theta[role]
        pack(res_send.at[role], residual.astype(bf16))

        @pl.when(has_lo)
        def _():
            res_copy(role, 0).start()

        @pl.when(has_hi)
        def _():
            res_copy(role, 1).start()

        return residual

    residual = send_res(upper)

    @pl.when(has_up)
    def _():
        image[lower] = send_res(lower)
        lax.fori_loop(0, chunks, lower_step, 0)

    def overlap(role, own):
        theta_out[...] = own * slab(role, 1)

        @pl.when(has_hi)
        def _():
            res_copy(role, 0).wait_recv()
            above = unpack(res_recv.at[role, 0], size).astype(f32)
            theta_out[...] = theta_out[...] + above * slab(role, 2)

        @pl.when(has_lo)
        def _():
            res_copy(role, 1).wait_recv()
            below = unpack(res_recv.at[role, 1], size).astype(f32)
            theta_out[...] = theta_out[...] + below * slab(role, 0)

        return column_sums(theta_out[...])

    def low_copy(j):
        return remote(
            low_send, low_recv.at[q], low_s.at[j], low_r.at[q], seg=up, grp=j)

    def low_incoming(j):
        return remote(low_send, low_recv.at[j], low_s.at[j], low_r.at[j], seg=dn, grp=j)

    @pl.when(has_up)
    def _():
        zero = jnp.zeros((1, size), f32)
        low_send[...] = stat_tile([zero, zero, overlap(lower, image[lower])])
        for j in range(grps):
            low_copy(j).start()

    stat_start(
        2,
        [
            column_sums(residual * residual),
            column_sums(residual * image[upper]),
            overlap(upper, residual),
        ],
    )

    @pl.when(has_dn)
    def _():
        for j in range(grps):
            low_incoming(j).wait_recv()

    @pl.when(jnp.logical_not(has_dn))
    def _():
        low_recv[...] = jnp.zeros(low_recv.shape, f32)

    sums = total(stat_finish(2), low_recv)
    scale = 1.0 / jnp.sqrt(sums[0:1, :] + eps_value)
    coupling = sums[1:2, :] * scale
    diag_two = (sums[2:3, :] - diag_one * sums[1:2, :]) * scale * scale
    half_gap = 0.5 * (diag_one - diag_two)
    energy = 0.5 * (diag_one + diag_two) - jnp.sqrt(half_gap * half_gap + coupling * coupling)
    lead_coef = diag_two - energy
    norm_scale = jnp.sqrt(lead_coef * lead_coef + coupling * coupling)
    energy_out[...] = energy
    theta_out[...] = (lead_coef * theta[upper] - coupling * (residual * scale)) / norm_scale

    @pl.when(has_up)
    def _():
        site_up().wait_send()
        z_copy(lower).wait_send()
        for k in range(chunks):
            env_up(k).wait_send()
        for j in range(grps):
            low_copy(j).wait_send()

    @pl.when(has_dn)
    def _():
        site_dn().wait_send()
        ch_dn().wait_send()
        z_copy(upper).wait_send()
        for k in range(chunks):
            env_dn(k).wait_send()

    for slot in range(3):
        for d in range(1, grps):
            stat_copy(slot, d).wait_send()

    def drain(role):
        @pl.when(has_lo)
        def _():
            slab_copy(role, 0).wait_send()
            res_copy(role, 0).wait_send()

        @pl.when(has_hi)
        def _():
            slab_copy(role, 1).wait_send()
            res_copy(role, 1).wait_send()

    drain(upper)

    @pl.when(has_up)
    def _():
        drain(lower)


def body(env_left, env_right, site_left, site_right, bond_weights, mpo_charge, sector_rows):
    width, size = env_left.shape[2:4]
    segs, grps = lax.axis_size("seg"), lax.axis_size("grp")
    half = width // 2
    chunk = 3 if half % 3 == 0 else 1
    chunks = half // chunk
    tall = size + size // 2
    charge_rows = (width // 8 + 1) * 8
    vmem = pl.BlockSpec(memory_space=pltpu.VMEM)
    hbm = pl.BlockSpec(memory_space=pltpu.HBM)
    dma = pltpu.SemaphoreType.DMA
    theta_new, energy = pl.pallas_call(
        functools.partial(kernel, segs, grps, chunk),
        out_shape=(
            jax.ShapeDtypeStruct((size, size), f32),
            jax.ShapeDtypeStruct((1, 1), f32),
        ),
        in_specs=[hbm] * 7,
        out_specs=(vmem, vmem),
        scratch_shapes=[
            pltpu.VMEM((size, size), bf16),
            pltpu.VMEM((size, size), bf16),
            pltpu.VMEM((1, size), f32),
            pltpu.SMEM(mpo_charge.shape, jnp.int32),
            pltpu.SMEM(sector_rows.shape, jnp.int32),
            pltpu.VMEM((width, size, size), bf16),
            pltpu.VMEM((width, size, size), bf16),
            pltpu.VMEM((chunks, chunk, tall, lanes), bf16),
            pltpu.VMEM((chunks, chunk, tall, lanes), bf16),
            pltpu.VMEM((chunks, chunk, tall, lanes), bf16),
            pltpu.VMEM((chunks, chunk, tall, lanes), bf16),
            pltpu.VMEM((half, size, size), bf16),
            pltpu.VMEM((half, size, size), bf16),
            pltpu.VMEM((2, tall, lanes), bf16),
            pltpu.VMEM((2, tall, lanes), bf16),
            pltpu.VMEM((charge_rows, size), f32),
            pltpu.VMEM((charge_rows, size), f32),
            pltpu.VMEM((2, size, size), f32),
            pltpu.VMEM((2, size, size), bf16),
            pltpu.VMEM((2, size, size), f32),
            pltpu.VMEM((2, 3 * size, size), f32),
            pltpu.VMEM((2, 2, tall, lanes), bf16),
            pltpu.VMEM((2, 2, tall, lanes), bf16),
            pltpu.VMEM((2, tall, lanes), bf16),
            pltpu.VMEM((2, tall, lanes), bf16),
            pltpu.VMEM((2, tall, lanes), bf16),
            pltpu.VMEM((2, 2, tall, lanes), bf16),
            pltpu.VMEM((3, 8, size), f32),
            pltpu.VMEM((3, grps, 8, size), f32),
            pltpu.VMEM((8, size), f32),
            pltpu.VMEM((grps, 8, size), f32),
            dma((2 * chunks + 7,)),
            dma((2, chunks)),
            dma((2, chunks)),
            dma((3,)),
            dma((3,)),
            dma((2, 2)),
            dma((2, 2)),
            dma((2,)),
            dma((2,)),
            dma((2, 2)),
            dma((2, 2)),
            dma((3, grps)),
            dma((3, grps)),
            dma((grps,)),
            dma((grps,)),
        ],
        compiler_params=pltpu.CompilerParams(
            collective_id=0, has_side_effects=True, vmem_limit_bytes=62 * 1024 * 1024
        ),
        cost_estimate=pl.CostEstimate(
            flops=16 * width * size**3, bytes_accessed=4 * width * size * size, transcendentals=0
        ),
    )(
        env_left[0, 0],
        env_right[0, 0],
        site_left[0, 0],
        site_right[0, 0],
        bond_weights[0],
        mpo_charge,
        sector_rows,
    )
    return (theta_new[None, None], energy[0])


def solution(mesh):
    return jax.shard_map(
        body,
        mesh=mesh,
        in_specs=(
            P(("parts", "seg"), "grp", None, None, None),
            P(("parts", "seg"), "grp", None, None, None),
            P(("parts", "seg"), "grp", None, None),
            P(("parts", "seg"), "grp", None, None),
            P(("parts", "seg"), "grp", None),
            P(("parts", "seg"), None),
            P(("parts", "seg"), "grp"),
        ),
        out_specs=(P(("parts", "seg"), "grp", None, None), P(("parts", "seg"))),
        check_vma=False,
    )
```

```python
import functools

import jax
import jax.numpy as jnp
from jax import lax
from jax.experimental import pallas as pl
from jax.experimental.pallas import tpu as pltpu
from jax.sharding import PartitionSpec as P

eps_value = 1e-06
lanes = 128
f32 = jnp.float32
bf16 = jnp.bfloat16


def pack(dst, x):
    size = x.shape[0]
    half, rest = size // 2, size - lanes
    dst[0:size, :] = x[:, :lanes]
    dst[size : size + half, :] = jnp.concatenate([x[:half, lanes:], x[half:, lanes:]], axis=1)


def unpack(src, size):
    half, rest = size // 2, size - lanes
    tail = src[size : size + half, :]
    tall = jnp.concatenate([tail[:, :rest], tail[:, rest:]], axis=0)
    return jnp.concatenate([src[0:size, :], tall], axis=1)


def kernel(
    segs, grps, chunk,
    el, er, sl_in, sr_in, bw_in, chg_in, rows_in,
    theta_out, energy_out,
    sl, sr, bw, chg, rows, elv, erv, send_a, send_b, recv_a, recv_b, full_a, full_b,
    site_send, site_recv, ch_loc, ch_rem,
    theta, v16, image, acc,
    slab_send, slab_recv, z_send, z_recv, res_send, res_recv,
    stat_send, stat_recv, low_send, low_recv,
    loc_sem, env_s, env_r, site_s, site_r, slab_s, slab_r,
    z_s, z_r, res_s, res_r, stat_s, stat_r, low_s, low_r,
):
    width, size, _ = el.shape
    half = width // 2
    chunks = half // chunk
    entry_count = float(grps * size * size)
    s = lax.axis_index("seg")
    q = lax.axis_index("grp")
    has_up = s < segs - 1
    has_dn = s > 0
    has_hi = q < grps - 1
    has_lo = q > 0
    up, dn = jnp.minimum(s + 1, segs - 1), jnp.maximum(s - 1, 0)
    hi, lo = jnp.minimum(q + 1, grps - 1), jnp.maximum(q - 1, 0)
    upper, lower = 0, 1

    def remote(src, dst, ssem, rsem, **where):
        return pltpu.make_async_remote_copy(
            src_ref=src, dst_ref=dst, send_sem=ssem, recv_sem=rsem,
            device_id=where, device_id_type=pl.DeviceIdType.MESH,
        )

    def load_a(k):
        at = pl.ds(k * chunk, chunk)
        return pltpu.make_async_copy(el.at[at], elv.at[at], loc_sem.at[k])

    def load_b(k):
        at = pl.ds(half + k * chunk, chunk)
        return pltpu.make_async_copy(er.at[at], erv.at[at], loc_sem.at[chunks + k])

    def load_rest_a():
        at = pl.ds(half, half)
        return pltpu.make_async_copy(el.at[at], elv.at[at], loc_sem.at[2 * chunks])

    def load_rest_b():
        at = pl.ds(0, half)
        return pltpu.make_async_copy(er.at[at], erv.at[at], loc_sem.at[2 * chunks + 1])

    small = [
        pltpu.make_async_copy(src, dst, loc_sem.at[2 * chunks + 2 + i])
        for i, (src, dst) in enumerate(
            ((sl_in, sl), (bw_in, bw), (sr_in, sr), (chg_in, chg), (rows_in, rows)))
    ]
    for copy in small:
        copy.start()
    for k in range(chunks):
        load_a(k).start()
        load_b(k).start()
    load_rest_a().start()
    load_rest_b().start()

    barrier = pltpu.get_barrier_semaphore()
    for d in range(1, grps):
        pl.semaphore_signal(
            barrier, inc=1, device_id={"grp": lax.rem(q + d, grps)},
            device_id_type=pl.DeviceIdType.MESH)

    @pl.when(has_up)
    def _():
        for j in range(grps):
            pl.semaphore_signal(
                barrier, inc=1, device_id={"seg": up, "grp": j},
                device_id_type=pl.DeviceIdType.MESH)

    @pl.when(has_dn)
    def _():
        for j in range(grps):
            pl.semaphore_signal(
                barrier, inc=1, device_id={"seg": dn, "grp": j},
                device_id_type=pl.DeviceIdType.MESH)

    for copy in small:
        copy.wait()
    scaled = (sl[...].astype(f32) / bw[...]).astype(bf16)
    site_right = sr[...]
    pack(site_send.at[0], scaled)
    pack(site_send.at[1], site_right)
    for w in range(width):
        ch_loc[w : w + 1, :] = jnp.full((1, size), chg[0, w], jnp.int32).astype(f32)
    pad = ch_loc.shape[0] - width
    ch_loc[width:, :] = jnp.full((pad, size), rows[0, 0], jnp.int32).astype(f32)

    def pack_chunk(k, carry):
        load_a(k).wait()
        load_b(k).wait()
        for j in range(chunk):
            pack(send_a.at[k, j], elv[k * chunk + j])
            pack(send_b.at[k, j], erv[half + k * chunk + j])
        return carry

    lax.fori_loop(0, chunks, pack_chunk, 0)
    load_rest_a().wait()
    load_rest_b().wait()

    row_at = lax.broadcasted_iota(jnp.int32, (size, size), 0)
    col_at = lax.broadcasted_iota(jnp.int32, (size, size), 1)
    eye_block = jnp.where(row_at == col_at, 1.0, 0.0)

    @pl.when(jnp.logical_not(has_dn))
    def _():
        for w in range(half):
            full_a[w] = (eye_block if w == 0 else jnp.zeros_like(eye_block)).astype(bf16)

    for i in (upper, lower):
        acc[i] = jnp.zeros(acc.shape[1:], f32)

    pl.semaphore_wait(
        barrier, grps - 1 + grps * (has_up.astype(jnp.int32) + has_dn.astype(jnp.int32)))

    def site_up():
        return remote(site_send.at[0], site_recv.at[0], site_s.at[0], site_r.at[0], seg=up)

    def site_dn():
        return remote(site_send.at[1], site_recv.at[1], site_s.at[1], site_r.at[1], seg=dn)

    def ch_dn():
        return remote(ch_loc, ch_rem, site_s.at[2], site_r.at[2], seg=dn)

    def env_up(k):
        return remote(send_a.at[k], recv_a.at[k], env_s.at[0, k], env_r.at[0, k], seg=up)

    def env_dn(k):
        return remote(send_b.at[k], recv_b.at[k], env_s.at[1, k], env_r.at[1, k], seg=dn)

    @pl.when(has_up)
    def _():
        site_up().start()

    @pl.when(has_dn)
    def _():
        site_dn().start()
        ch_dn().start()

    def send_chunk(k, carry):
        @pl.when(has_up)
        def _():
            env_up(k).start()

        @pl.when(has_dn)
        def _():
            env_dn(k).start()

        return carry

    lax.fori_loop(0, chunks, send_chunk, 0)

    row_f = row_at.astype(f32)

    def live(ch):
        return jnp.where(row_f < ch[width : width + 1, :], 1.0, 0.0)

    @pl.when(has_dn)
    def _():
        site_up().wait_recv()
        edge = unpack(site_recv.at[0], size)
        theta[upper] = jnp.dot(edge, site_right, preferred_element_type=f32) * live(ch_loc)

    @pl.when(jnp.logical_not(has_dn))
    def _():
        theta[upper] = site_right.astype(f32) * live(ch_loc)

    @pl.when(has_up)
    def _():
        site_dn().wait_recv()
        ch_dn().wait_recv()
        above = unpack(site_recv.at[1], size)
        theta[lower] = jnp.dot(scaled, above, preferred_element_type=f32) * live(ch_rem)

    @pl.when(jnp.logical_not(has_up))
    def _():
        theta[lower] = jnp.zeros((size, size), f32)

    def column_sums(x):
        return jnp.sum(x, axis=0, keepdims=True)

    def stat_copy(slot, d):
        return remote(
            stat_send.at[slot], stat_recv.at[slot, q], stat_s.at[slot, d], stat_r.at[slot, d],
            grp=lax.rem(q + d, grps))

    def stat_tile(values):
        at = lax.broadcasted_iota(jnp.int32, (8, size), 0)
        tile = jnp.zeros((8, size), f32)
        for i, value in enumerate(values):
            tile = jnp.where(at == i, value, tile)
        return tile

    def stat_start(slot, values):
        tile = stat_tile(values)
        stat_send[slot] = tile
        stat_recv[slot, q] = tile
        for d in range(1, grps):
            stat_copy(slot, d).start()

    def total(tiles, extra=None):
        tile = tiles[0]
        for j in range(1, grps):
            tile = tile + tiles[j]
        if extra is not None:
            for j in range(grps):
                tile = tile + extra[j]
        return jnp.sum(tile, axis=1, keepdims=True) / entry_count

    def stat_finish(slot):
        for d in range(1, grps):
            stat_copy(slot, d).wait_recv()
        return stat_recv.at[slot]

    stat_start(0, [column_sums(theta[i] * theta[i]) for i in (upper, lower)])
    norms = total(stat_finish(0))
    for i in (upper, lower):
        basis = theta[i] / jnp.sqrt(norms[i : i + 1, :] + eps_value)
        theta[i] = basis
        v16[i] = basis.astype(bf16)

    def one_term(a, v, ch_row, b):
        inner = jnp.dot(a, v, preferred_element_type=f32).astype(bf16)
        parts = [inner * jnp.where(ch_row == c, 1.0, 0.0).astype(bf16) for c in (-1.0, 0.0, 1.0)]
        return jnp.dot(jnp.concatenate(parts, axis=0), b, preferred_element_type=f32)

    def upper_chunk(k, chunk=chunk):
        value = None
        for j in range(chunk):
            w = k * chunk + j
            term = one_term(full_a[w], v16[upper], ch_loc[pl.ds(w, 1), :], erv[w])
            value = term if value is None else value + term
        acc[upper] = acc[upper] + value

    def lower_chunk(k, chunk=chunk):
        value = None
        for j in range(chunk):
            w = k * chunk + j
            term = one_term(elv[half + w], v16[lower], ch_rem[pl.ds(half + w, 1), :], full_b[w])
            value = term if value is None else value + term
        acc[lower] = acc[lower] + value

    def first_chunk(k, carry):
        @pl.when(has_dn)
        def _():
            env_up(k).wait_recv()
            for j in range(chunk):
                full_a[k * chunk + j] = unpack(recv_a.at[k, j], size)

        upper_chunk(k)

        @pl.when(has_up)
        def _():
            env_dn(k).wait_recv()
            for j in range(chunk):
                full_b[k * chunk + j] = unpack(recv_b.at[k, j], size)
            lower_chunk(k)

        return carry

    lax.fori_loop(0, chunks, first_chunk, 0)

    def slab_copy(role, way):
        return remote(
            slab_send.at[role, way], slab_recv.at[role, way], slab_s.at[role, way],
            slab_r.at[role, way], grp=(lo, hi)[way])

    def res_copy(role, way):
        return remote(
            res_send.at[role], res_recv.at[role, way], res_s.at[role, way],
            res_r.at[role, way], grp=(lo, hi)[way])

    def z_copy(role):
        return remote(
            z_send.at[role], z_recv.at[1 - role], z_s.at[role], z_r.at[1 - role],
            seg=(dn, up)[role])

    def z_incoming(role):
        return remote(
            z_send.at[role], z_recv.at[role], z_s.at[role], z_r.at[role],
            seg=(dn, up)[role])

    def slab(role, c):
        return acc[role, c * size : (c + 1) * size, :]

    def send_slabs(role):
        @pl.when(has_lo)
        def _():
            pack(slab_send.at[role, 0], slab(role, 0).astype(bf16))
            slab_copy(role, 0).start()

        @pl.when(has_hi)
        def _():
            pack(slab_send.at[role, 1], slab(role, 2).astype(bf16))
            slab_copy(role, 1).start()

    def join_slabs(role, ch):
        image[role] = slab(role, 1).astype(bf16).astype(f32)

        @pl.when(has_hi)
        def _():
            slab_copy(role, 0).wait_recv()
            image[role] = image[role] + unpack(slab_recv.at[role, 0], size).astype(f32)

        @pl.when(has_lo)
        def _():
            slab_copy(role, 1).wait_recv()
            image[role] = image[role] + unpack(slab_recv.at[role, 1], size).astype(f32)

        half_image = (image[role] * live(ch)).astype(bf16)
        pack(z_send.at[role], half_image)
        z_copy(role).start()
        image[role] = half_image.astype(f32)

    send_slabs(upper)

    @pl.when(has_up)
    def _():
        send_slabs(lower)

    @pl.when(has_dn)
    def _():
        join_slabs(upper, ch_loc)

    @pl.when(jnp.logical_not(has_dn))
    def _():
        image[upper] = slab(upper, 1).astype(bf16).astype(f32)

        @pl.when(has_hi)
        def _():
            slab_copy(upper, 0).wait_recv()
            image[upper] = image[upper] + unpack(slab_recv.at[upper, 0], size).astype(f32)

        @pl.when(has_lo)
        def _():
            slab_copy(upper, 1).wait_recv()
            image[upper] = image[upper] + unpack(slab_recv.at[upper, 1], size).astype(f32)

        image[upper] = image[upper] * live(ch_loc)

    @pl.when(has_up)
    def _():
        join_slabs(lower, ch_rem)

    @pl.when(jnp.logical_not(has_up))
    def _():
        image[lower] = jnp.zeros((size, size), f32)

    @pl.when(has_dn)
    def _():
        z_incoming(upper).wait_recv()
        image[upper] = image[upper] + unpack(z_recv.at[upper], size).astype(f32)

    @pl.when(has_up)
    def _():
        z_incoming(lower).wait_recv()
        image[lower] = image[lower] + unpack(z_recv.at[lower], size).astype(f32)

    stat_start(1, [column_sums(theta[i] * image[i]) for i in (upper, lower)])
    for i in (upper, lower):
        v16[i] = image[i].astype(bf16)
        acc[i] = jnp.zeros(acc.shape[1:], f32)

    step = 5 if half % 5 == 0 else 1

    def upper_step(k, carry):
        upper_chunk(k, step)
        return carry

    def lower_step(k, carry):
        lower_chunk(k, step)
        return carry

    lax.fori_loop(0, half // step, upper_step, 0)

    diags = total(stat_finish(1))
    diag_one = diags[0:1, :]

    def send_res(role):
        residual = image[role] - diags[role : role + 1, :] * theta[role]
        pack(res_send.at[role], residual.astype(bf16))

        @pl.when(has_lo)
        def _():
            res_copy(role, 0).start()

        @pl.when(has_hi)
        def _():
            res_copy(role, 1).start()

        return residual

    residual = send_res(upper)

    @pl.when(has_up)
    def _():
        image[lower] = send_res(lower)
        lax.fori_loop(0, half // step, lower_step, 0)

    def overlap(role, own):
        theta_out[...] = own * slab(role, 1)

        @pl.when(has_hi)
        def _():
            res_copy(role, 0).wait_recv()
            above = unpack(res_recv.at[role, 0], size).astype(f32)
            theta_out[...] = theta_out[...] + above * slab(role, 2)

        @pl.when(has_lo)
        def _():
            res_copy(role, 1).wait_recv()
            below = unpack(res_recv.at[role, 1], size).astype(f32)
            theta_out[...] = theta_out[...] + below * slab(role, 0)

        return column_sums(theta_out[...])

    def low_copy(j):
        return remote(
            low_send, low_recv.at[q], low_s.at[j], low_r.at[q], seg=up, grp=j)

    def low_incoming(j):
        return remote(low_send, low_recv.at[j], low_s.at[j], low_r.at[j], seg=dn, grp=j)

    @pl.when(has_up)
    def _():
        zero = jnp.zeros((1, size), f32)
        low_send[...] = stat_tile([zero, zero, overlap(lower, image[lower])])
        for j in range(grps):
            low_copy(j).start()

    stat_start(
        2,
        [
            column_sums(residual * residual),
            column_sums(residual * image[upper]),
            overlap(upper, residual),
        ],
    )

    @pl.when(has_dn)
    def _():
        for j in range(grps):
            low_incoming(j).wait_recv()

    @pl.when(jnp.logical_not(has_dn))
    def _():
        low_recv[...] = jnp.zeros(low_recv.shape, f32)

    sums = total(stat_finish(2), low_recv)
    scale = 1.0 / jnp.sqrt(sums[0:1, :] + eps_value)
    coupling = sums[1:2, :] * scale
    diag_two = (sums[2:3, :] - diag_one * sums[1:2, :]) * scale * scale
    half_gap = 0.5 * (diag_one - diag_two)
    energy = 0.5 * (diag_one + diag_two) - jnp.sqrt(half_gap * half_gap + coupling * coupling)
    lead_coef = diag_two - energy
    norm_scale = jnp.sqrt(lead_coef * lead_coef + coupling * coupling)
    energy_out[...] = energy
    theta_out[...] = (lead_coef * theta[upper] - coupling * (residual * scale)) / norm_scale

    @pl.when(has_up)
    def _():
        site_up().wait_send()
        z_copy(lower).wait_send()
        for k in range(chunks):
            env_up(k).wait_send()
        for j in range(grps):
            low_copy(j).wait_send()

    @pl.when(has_dn)
    def _():
        site_dn().wait_send()
        ch_dn().wait_send()
        z_copy(upper).wait_send()
        for k in range(chunks):
            env_dn(k).wait_send()

    for slot in range(3):
        for d in range(1, grps):
            stat_copy(slot, d).wait_send()

    def drain(role):
        @pl.when(has_lo)
        def _():
            slab_copy(role, 0).wait_send()
            res_copy(role, 0).wait_send()

        @pl.when(has_hi)
        def _():
            slab_copy(role, 1).wait_send()
            res_copy(role, 1).wait_send()

    drain(upper)

    @pl.when(has_up)
    def _():
        drain(lower)


def body(env_left, env_right, site_left, site_right, bond_weights, mpo_charge, sector_rows):
    width, size = env_left.shape[2:4]
    segs, grps = lax.axis_size("seg"), lax.axis_size("grp")
    half = width // 2
    chunk = 3 if half % 3 == 0 else 1
    chunks = half // chunk
    tall = size + size // 2
    charge_rows = (width // 8 + 1) * 8
    vmem = pl.BlockSpec(memory_space=pltpu.VMEM)
    hbm = pl.BlockSpec(memory_space=pltpu.HBM)
    dma = pltpu.SemaphoreType.DMA
    theta_new, energy = pl.pallas_call(
        functools.partial(kernel, segs, grps, chunk),
        out_shape=(
            jax.ShapeDtypeStruct((size, size), f32),
            jax.ShapeDtypeStruct((1, 1), f32),
        ),
        in_specs=[hbm] * 7,
        out_specs=(vmem, vmem),
        scratch_shapes=[
            pltpu.VMEM((size, size), bf16),
            pltpu.VMEM((size, size), bf16),
            pltpu.VMEM((1, size), f32),
            pltpu.SMEM(mpo_charge.shape, jnp.int32),
            pltpu.SMEM(sector_rows.shape, jnp.int32),
            pltpu.VMEM((width, size, size), bf16),
            pltpu.VMEM((width, size, size), bf16),
            pltpu.VMEM((chunks, chunk, tall, lanes), bf16),
            pltpu.VMEM((chunks, chunk, tall, lanes), bf16),
            pltpu.VMEM((chunks, chunk, tall, lanes), bf16),
            pltpu.VMEM((chunks, chunk, tall, lanes), bf16),
            pltpu.VMEM((half, size, size), bf16),
            pltpu.VMEM((half, size, size), bf16),
            pltpu.VMEM((2, tall, lanes), bf16),
            pltpu.VMEM((2, tall, lanes), bf16),
            pltpu.VMEM((charge_rows, size), f32),
            pltpu.VMEM((charge_rows, size), f32),
            pltpu.VMEM((2, size, size), f32),
            pltpu.VMEM((2, size, size), bf16),
            pltpu.VMEM((2, size, size), f32),
            pltpu.VMEM((2, 3 * size, size), f32),
            pltpu.VMEM((2, 2, tall, lanes), bf16),
            pltpu.VMEM((2, 2, tall, lanes), bf16),
            pltpu.VMEM((2, tall, lanes), bf16),
            pltpu.VMEM((2, tall, lanes), bf16),
            pltpu.VMEM((2, tall, lanes), bf16),
            pltpu.VMEM((2, 2, tall, lanes), bf16),
            pltpu.VMEM((3, 8, size), f32),
            pltpu.VMEM((3, grps, 8, size), f32),
            pltpu.VMEM((8, size), f32),
            pltpu.VMEM((grps, 8, size), f32),
            dma((2 * chunks + 7,)),
            dma((2, chunks)),
            dma((2, chunks)),
            dma((3,)),
            dma((3,)),
            dma((2, 2)),
            dma((2, 2)),
            dma((2,)),
            dma((2,)),
            dma((2, 2)),
            dma((2, 2)),
            dma((3, grps)),
            dma((3, grps)),
            dma((grps,)),
            dma((grps,)),
        ],
        compiler_params=pltpu.CompilerParams(
            collective_id=0, has_side_effects=True, vmem_limit_bytes=62 * 1024 * 1024
        ),
        cost_estimate=pl.CostEstimate(
            flops=16 * width * size**3, bytes_accessed=4 * width * size * size, transcendentals=0
        ),
    )(
        env_left[0, 0],
        env_right[0, 0],
        site_left[0, 0],
        site_right[0, 0],
        bond_weights[0],
        mpo_charge,
        sector_rows,
    )
    return (theta_new[None, None], energy[0])


def solution(mesh):
    return jax.shard_map(
        body,
        mesh=mesh,
        in_specs=(
            P(("parts", "seg"), "grp", None, None, None),
            P(("parts", "seg"), "grp", None, None, None),
            P(("parts", "seg"), "grp", None, None),
            P(("parts", "seg"), "grp", None, None),
            P(("parts", "seg"), "grp", None),
            P(("parts", "seg"), None),
            P(("parts", "seg"), "grp"),
        ),
        out_specs=(P(("parts", "seg"), "grp", None, None), P(("parts", "seg"))),
        check_vma=False,
    )
```
